32 devices in a mesh: row: 4 (over z), depth: 8 (over y, x, core).
Axes of the slice: x: 2, y: 2, z: 4, core: 2. Of those that a mesh axis runs over, the one named last changes fastest.
Arguments:
- table: float32 [4, 1024, 256], P(None, 'row'), may hold values from -6 to 6
- accum: float32 [4, 1024], P(None, 'row'), may hold values from 0.0001 to 0.01
- owner: int32 [256, 4, 64, 1], P(('row', 'depth')), may hold values from 0 to 3; in each aligned block of 2048 rows (0 to 2047, 2048 to 4095, ..., all dimensions but the last counted through in order) at most 1024 rows name the same one
- local_row: int32 [256, 4, 64], P(('row', 'depth')), may hold values from 0 to 255
- lengths: int32 [256, 4], P(('row', 'depth')), may hold values from 1 to 64
- dense_q: int32 [256, 13], P(('row', 'depth')), may hold values from 0 to 255
- labels: int32 [256], P(('row', 'depth')), may hold values 0 or 1
- bottom_w: float32 [13, 256], replicated, may hold values from -1.75 to 1.75
- top_w: float32 [10], replicated, may hold values from -4 to 4
Outputs:
- new_table: float32 [4, 1024, 256], P(None, 'row')
- new_accum: float32 [4, 1024], P(None, 'row')
- logits: float32 [256], P(('row', 'depth'))
The draws below stay inside these ranges and needn't reach their ends.
Inputs may be any that keep to these rules, and one draw needn't show every extreme that they name: `owner`: among the id slots of one device (aligned blocks of 2048 slots, padding slots included), no value is named more than 1024 times, a bound that some block reaches.
All inputs are finite; a program needn't handle non-finite values. No bound on the sum of `labels` on one device may be relied on, other than what follows from the above.
Results may differ from the reference program's by a relative error of at most 0.00012.
Values sent between devices are 32-bit elements; how exact they have to be, the bound alone decides.
A program may use at most 64 MiB of HBM per device.

```python
import math
import jax
import jax.numpy as jnp
import numpy as np
from jax import lax

TABLES = 4
W = 256
DENSE = 13
PAIRS = 10
BAG = 64
ROWS_DEV = 256
SAMP_DEV = 8
ROWS = 1024
BATCH = 256
CAP = 1024
N_ROW = 4


def plant(drawn, own_key, least, high):
    dims = drawn.shape
    place = [jax.random.randint(jax.random.fold_in(own_key, axis), (), 0, dims[axis]) for axis in range(len(dims))]
    drawn = drawn.at[tuple(place)].set(least)
    longest = dims.index(max(dims))
    place[longest] = (place[longest] + 1) % dims[longest]
    return drawn.at[tuple(place)].set(high)


def shard_levels(key, dims, shards, smallest, largest):
    def one(position, parts):
        steps = jax.random.uniform(jax.random.fold_in(jax.random.fold_in(key, 6), position), (parts,), jnp.float32, smallest / len(shards), largest / len(shards))
        return jnp.repeat(jnp.exp(steps), dims[position] // parts).reshape((-1,) + (1,) * (len(dims) - position - 1))

    loudness = one(*shards[0])
    for cut in shards[1:]:
        loudness = loudness * one(*cut)
    return loudness


def routed_block(rng, own, number, rows, amount, top, reach, lean):
    order = jax.random.permutation(rng, amount)
    heavy_load, usual = shares(amount, rows * top, reach, lean, True), shares(amount, rows * top, reach, lean, False)
    places = jnp.arange(amount)

    def named(tallies, offset_by):
        used = int((tallies > 0).sum())
        fixed = max(1, used // 4)
        passed = fixed + (places - fixed + offset_by * (used - fixed)) % max(1, amount - fixed)
        return jnp.zeros((amount,), jnp.int32).at[order[jnp.where(places < fixed, places, passed)]].set(jnp.asarray(tallies, jnp.int32))

    tallies = jnp.where(number % 4 == 0, named(heavy_load, number // 4), named(usual, number - number // 4 - 1))
    mixed = jax.random.permutation(jax.random.fold_in(own, 3), amount)
    source_of, receiver = mixed[0:amount // 2 * 2:2], mixed[1:amount // 2 * 2:2]
    slack = jnp.minimum(tallies[source_of] - 1, reach - tallies[receiver]) // 2
    slack = jnp.where((source_of == order[0]) | (receiver == order[0]) | (tallies[receiver] == 0), 0, jnp.maximum(slack, 0))
    passed = jax.random.randint(jax.random.fold_in(own, 4), (amount // 2,), 0, 1 << 20) % (slack + 1)
    tallies = tallies.at[source_of].add(-passed).at[receiver].add(passed)
    items = jnp.searchsorted(jnp.cumsum(tallies), jnp.arange(rows * top), side="right").astype(jnp.int32)
    grid = items.reshape(top, rows).T
    grid = grid[jax.random.permutation(jax.random.fold_in(own, 1), rows)]
    offset_by = jax.random.randint(jax.random.fold_in(own, 2), (rows, 1), 0, top)
    return jnp.take_along_axis(grid, (jnp.arange(top)[None, :] + offset_by) % top, axis=1)


def shares(amount, total, reach, skew, full):
    portions = [(1 << 20) // math.isqrt(standing ** skew) + 1 for standing in range(1, amount + 1)]
    largest = reach if full else min(reach, max(-(-total // amount), total * portions[0] // sum(portions)))
    least = 1 if total - largest >= amount - 1 else 0
    given, spare = [largest] + [least] * (amount - 1), total - largest - least * (amount - 1)
    while spare > 0:
        candidates = [i for i in range(1, amount) if given[i] < largest] or [i for i in range(1, amount) if given[i] < reach]
        whole, left = sum([portions[i] for i in candidates]), spare
        for i in candidates:
            extra = min(reach - given[i], max(1, left * portions[i] // whole), spare)
            given[i] = given[i] + extra
            spare = spare - extra
    return np.array(given)


def gaussian(rng, extent, deviation, bound, shards=(), kind=jnp.bfloat16):
    gain = shard_levels(rng, extent, shards, -0.22, 0.18) if shards else 1.0
    array = jax.random.normal(rng, extent, jnp.float32) * deviation * gain
    return jnp.minimum(jnp.maximum(array, -bound), bound).astype(kind)


def setup_inputs(seed: int = 0) -> dict:
    streams_of = jax.random.split(jax.random.key(seed), 10)
    table = gaussian(streams_of[0], (TABLES, ROWS, W), 1.0, 6.0, ((1, 4),), jnp.float32)
    accum = jnp.clip(jnp.exp(math.log(0.01) - 4.6051702 * jax.random.uniform(streams_of[1], (TABLES, ROWS), jnp.float32) ** shard_levels(streams_of[1], (TABLES, ROWS), ((1, 4),), -0.2, 0.2)), 0.0001, 0.01)
    owner_keys = jax.random.split(jax.random.fold_in(streams_of[2], 1), BATCH * TABLES * BAG // (SAMP_DEV * TABLES * BAG))
    owner_turns = jax.random.permutation(jax.random.fold_in(streams_of[2], 3), BATCH * TABLES * BAG // (SAMP_DEV * TABLES * BAG))
    owner = jax.vmap(lambda own, number: routed_block(jax.random.fold_in(streams_of[2], 2), own, number, SAMP_DEV * TABLES * BAG, N_ROW, 1, CAP, 2))(owner_keys, owner_turns).reshape((BATCH, TABLES, BAG, 1))
    local_row = plant(jax.random.randint(streams_of[3], (BATCH, TABLES, BAG), 0, ROWS_DEV), jax.random.fold_in(streams_of[3], 1), 0, ROWS_DEV - 1).astype(jnp.int32)
    lengths = plant(jax.random.randint(streams_of[4], (BATCH, TABLES), 1, BAG + 1), jax.random.fold_in(streams_of[4], 1), 1, BAG).astype(jnp.int32)
    dense_q = plant(jax.random.randint(streams_of[5], (BATCH, DENSE), 0, 256), jax.random.fold_in(streams_of[5], 1), 0, 255).astype(jnp.int32)
    labels = plant((jax.random.randint(streams_of[6], (BATCH,), 0, 2) < 1).astype(jnp.int32), jax.random.fold_in(streams_of[6], 1), 0, 1)
    bottom_w = gaussian(streams_of[7], (DENSE, W), DENSE ** -0.5, 1.75, (), jnp.float32)
    top_w = gaussian(streams_of[8], (PAIRS,), 1.0, 4.0, (), jnp.float32)
    return {"table": table, "accum": accum, "owner": owner, "local_row": local_row, "lengths": lengths, "dense_q": dense_q, "labels": labels, "bottom_w": bottom_w, "top_w": top_w}


LEARN_RATE = 0.5
EPSILON = 1e-08

def pair_matrix(top_w, count):
    upper_i, upper_k = np.triu_indices(count, 1)
    matrix = jnp.zeros((count, count), jnp.float32)
    matrix = matrix.at[upper_i, upper_k].set(top_w)
    return matrix.at[upper_k, upper_i].set(top_w)

def reference(table, accum, owner, local_row, lengths, dense_q, labels, bottom_w, top_w):
    global_rows = owner[:, :, :, 0] * ROWS_DEV + local_row
    is_live = (lax.broadcasted_iota(jnp.int32, global_rows.shape, 2) < lengths[:, :, None]).astype(jnp.float32)
    batch_size = global_rows.shape[0]
    positions = jnp.arange(BAG, dtype=jnp.int32)
    pooled_list = []
    for table_at in range(TABLES):

        def add_position(pooled_sum, slot_at, table_at=table_at):
            row_index = lax.dynamic_index_in_dim(global_rows[:, table_at, :], slot_at, 1, keepdims=False)
            weight = lax.dynamic_index_in_dim(is_live[:, table_at, :], slot_at, 1, keepdims=False)
            return (pooled_sum + table[table_at][row_index] * weight[:, None], None)
        pooled_sum, unused = lax.scan(add_position, jnp.zeros((batch_size, W), jnp.float32), positions)
        pooled_list.append(pooled_sum)
    pooled = jnp.stack(pooled_list, 1)
    dequant = (dense_q.astype(jnp.float32) - 128.0) / 64.0
    dense_vec = jnp.dot(dequant, bottom_w, precision=lax.Precision.HIGHEST)
    bag_scale = float(BAG) ** (-0.5)
    width_scale = float(W) ** (-0.5)
    vectors = jnp.concatenate([dense_vec[:, None, :], bag_scale * pooled], axis=1)
    dots = width_scale * jnp.einsum('biw,bkw->bik', vectors, vectors, precision=lax.Precision.HIGHEST)
    matrix = pair_matrix(top_w, TABLES + 1)
    logits = 0.5 * lax.optimization_barrier(jnp.sum(dots * matrix[None, :, :], axis=(1, 2)))
    loss_coeff = (jax.nn.sigmoid(logits) - labels.astype(jnp.float32)) * bag_scale * width_scale
    mixed = jnp.einsum('ti,biw->btw', matrix[1:, :], vectors, precision=lax.Precision.HIGHEST)
    pooled_grad = loss_coeff[:, None, None] * mixed
    table_list = []
    accum_list = []
    for table_at in range(TABLES):

        def add_gradient(running, slot_at, table_at=table_at):
            row_index = lax.dynamic_index_in_dim(global_rows[:, table_at, :], slot_at, 1, keepdims=False)
            weight = lax.dynamic_index_in_dim(is_live[:, table_at, :], slot_at, 1, keepdims=False)
            return (running.at[row_index].add(pooled_grad[:, table_at, :] * weight[:, None]), None)
        row_grad, unused = lax.scan(add_gradient, jnp.zeros((ROWS, W), jnp.float32), positions)
        state = accum[table_at] + lax.optimization_barrier(jnp.mean(row_grad * row_grad, axis=1))
        table_list.append(table[table_at] - LEARN_RATE * row_grad / (jnp.sqrt(state)[:, None] + EPSILON))
        accum_list.append(state)
    return (jnp.stack(table_list, 0), jnp.stack(accum_list, 0), logits)
```

```python
import functools

import jax
import jax.numpy as jnp
import numpy as np
from jax import lax
from jax.experimental import pallas as pl
from jax.experimental.pallas import tpu as pltpu
from jax.sharding import PartitionSpec as P

LEARN_RATE = 0.5
EPSILON = 1e-08


def pair_matrix(top_w, count):
    upper_i, upper_k = np.triu_indices(count, 1)
    matrix = jnp.zeros((count, count), jnp.float32)
    matrix = matrix.at[upper_i, upper_k].set(top_w)
    return matrix.at[upper_k, upper_i].set(top_w)


def adagrad(rows_now, state_now, gradient):
    state = state_now + jnp.mean(gradient * gradient, axis=1)
    return (rows_now - LEARN_RATE * gradient / (jnp.sqrt(state)[:, None] + EPSILON), state)


def shards_large(table, accum, owner, local_row, lengths, dense_q, labels, bottom_w, top_w):
    tables, rows_dev, features = table.shape
    samples, bag_size = (owner.shape[0], owner.shape[2])
    row_devices = lax.axis_size("row")
    slot_count = samples * tables * bag_size
    bag_count = samples * tables
    capacity = 2 * slot_count // row_devices
    row_span = tables * rows_dev
    owner_of = owner.reshape(slot_count)
    local_of = local_row.reshape(slot_count)
    slot_live = (
        lax.broadcasted_iota(jnp.int32, (samples, tables, bag_size), 2) < lengths[:, :, None]
    ).reshape(slot_count)
    slot_index = jnp.arange(slot_count, dtype=jnp.int32)
    bag_of = slot_index // bag_size
    table_of = bag_of % tables
    entry_codes = jnp.where(slot_live, bag_of * row_span + table_of * rows_dev + local_of, -1)
    owner_hits = (owner_of[:, None] == jnp.arange(row_devices, dtype=jnp.int32)[None, :]).astype(
        jnp.int32
    )
    before = jnp.cumsum(owner_hits, axis=0) - owner_hits
    position = jnp.sum(before * owner_hits, axis=1)
    outgoing = (
        jnp.full((row_devices * capacity,), -1, jnp.int32)
        .at[owner_of * capacity + position]
        .set(entry_codes)
    )
    received = lax.all_to_all(
        outgoing.reshape(row_devices, capacity), "row", split_axis=0, concat_axis=0, tiled=True
    )
    is_live = received >= 0
    flat_rows = jnp.where(is_live, received % row_span, 0)
    bag_at = jnp.where(is_live, received // row_span, -1)
    flat_table = table.reshape(row_span, features)
    picked = flat_table[flat_rows]
    choose = (bag_at[:, None, :] == jnp.arange(bag_count, dtype=jnp.int32)[None, :, None]).astype(
        jnp.float32
    )
    partial_pool = jnp.einsum("sbc,scw->sbw", choose, picked, precision=lax.Precision.HIGHEST)
    returned = lax.all_to_all(partial_pool, "row", split_axis=0, concat_axis=0, tiled=True)
    pooled = jnp.sum(returned, axis=0).reshape(samples, tables, features)
    dequant = (dense_q.astype(jnp.float32) - 128.0) / 64.0
    dense_vec = jnp.dot(dequant, bottom_w, precision=lax.Precision.HIGHEST)
    bag_scale = float(bag_size) ** (-0.5)
    width_scale = float(features) ** (-0.5)
    vectors = jnp.concatenate([dense_vec[:, None, :], bag_scale * pooled], axis=1)
    dots = width_scale * jnp.einsum(
        "biw,bkw->bik", vectors, vectors, precision=lax.Precision.HIGHEST
    )
    matrix = pair_matrix(top_w, tables + 1)
    logits = 0.5 * jnp.sum(dots * matrix[None, :, :], axis=(1, 2))
    loss_coeff = (jax.nn.sigmoid(logits) - labels.astype(jnp.float32)) * bag_scale * width_scale
    mixed = jnp.einsum("ti,biw->btw", matrix[1:, :], vectors, precision=lax.Precision.HIGHEST)
    pooled_grad = (loss_coeff[:, None, None] * mixed).reshape(1, bag_count, features)
    piece = lax.all_gather(pooled_grad, "row", axis=0, tiled=True)
    piece_sources = piece.shape[0]
    piece_live = received >= 0
    piece_bags = jnp.where(piece_live, received // row_span, 0)
    source_at = jnp.arange(piece_sources, dtype=jnp.int32)[:, None]
    slot_grads = piece[source_at, piece_bags] * piece_live[:, :, None].astype(jnp.float32)
    row_grad = (
        jnp.zeros((row_span, features), jnp.float32)
        .at[flat_rows.reshape(-1)]
        .add(slot_grads.reshape(-1, features))
    )
    flat_accum = accum.reshape(row_span)
    summed = lax.psum(row_grad, "depth")
    new_rows, new_state = adagrad(flat_table, flat_accum, summed)
    return (
        new_rows.reshape(tables, rows_dev, features),
        new_state.reshape(tables, rows_dev),
        logits,
    )


def remote(src, dst, send_sem, recv_sem, device):
    return pltpu.make_async_remote_copy(
        src_ref=src,
        dst_ref=dst,
        send_sem=send_sem,
        recv_sem=recv_sem,
        device_id=device,
        device_id_type=pl.DeviceIdType.MESH,
    )


def two_terms(value):
    high = value.astype(jnp.bfloat16)
    return high, (value - high.astype(jnp.float32)).astype(jnp.bfloat16)


def matmul(a, b):
    return lax.dot_general(a, b, (((1,), (0,)), ((), ())), preferred_element_type=jnp.float32)


def step_kernel(
    table,
    accum,
    owner,
    local_row,
    lengths,
    dense_q,
    labels,
    bottom_w,
    top_w,
    new_table,
    new_accum,
    logits_out,
    codes,
    counts,
    partials,
    pools,
    grads,
    weights,
    state_cols,
    code_send,
    code_recv,
    count_send,
    count_pass,
    count_recv,
    pool_send,
    pool_recv,
    grad_send,
    grad_spread,
    grad_pass,
    grad_recv,
):
    rows = codes.shape[0]
    depths = counts.shape[0]
    half = depths // 2
    tables, rows_dev, features = table.shape
    samples, _, bag_size = owner.shape
    r = lax.axis_index("row")
    d = lax.axis_index("depth")
    partner = d + 1 - 2 * lax.rem(d, 2)
    row_peers = [lax.rem(r + k, rows) for k in range(1, rows)]
    depth_peers = [lax.rem(d + 2 * k, depths) for k in range(1, half)]
    partner_side = [partner] + [lax.rem(partner + 2 * k, depths) for k in range(1, half)]

    barrier = pltpu.get_barrier_semaphore()
    for peer in row_peers:
        pl.semaphore_signal(
            barrier, inc=1, device_id={"row": peer}, device_id_type=pl.DeviceIdType.MESH
        )
    for peer in depth_peers + [partner]:
        pl.semaphore_signal(
            barrier, inc=1, device_id={"depth": peer}, device_id_type=pl.DeviceIdType.MESH
        )

    slot_at = lax.broadcasted_iota(jnp.int32, (samples, bag_size), 1)
    mine = []
    for t in range(tables):
        live = slot_at < lengths[:, t : t + 1]
        mine.append(jnp.where(live, owner[:, t, :] * rows_dev + local_row[:, t, :], -1))
    for p in range(tables // 2):
        codes[r, p] = jnp.concatenate([mine[2 * p], mine[2 * p + 1]], axis=1)

    pl.semaphore_wait(barrier, rows - 1 + half)

    code_copies = [
        remote(codes.at[r], codes.at[r], code_send.at[i], code_recv.at[r], {"row": peer})
        for i, peer in enumerate(row_peers)
    ]
    for copy in code_copies:
        copy.start()

    row_at = lax.broadcasted_iota(jnp.int32, (samples, rows_dev), 1)

    def count(source):
        def pair(p, carry):
            relative = codes[source, p] - r * rows_dev
            for side in range(2):
                total = jnp.zeros((samples, rows_dev), jnp.float32)
                for j in range(bag_size):
                    at = side * bag_size + j
                    total = total + jnp.where(relative[:, at : at + 1] == row_at, 1.0, 0.0)
                counts[d, source, 2 * p + side] = total
            return carry

        lax.fori_loop(0, tables // 2, pair, 0)

    count(r)

    def count_peer(k, carry):
        source = lax.rem(r + k, rows)
        remote(
            codes.at[source], codes.at[source], code_send.at[0], code_recv.at[source], {"row": source}
        ).wait_recv()
        count(source)
        return carry

    lax.fori_loop(1, rows, count_peer, 0)

    count_copies = [
        remote(counts.at[d], counts.at[d], count_send.at[i], count_recv.at[d], {"depth": peer})
        for i, peer in enumerate(depth_peers)
    ]

    for t in range(tables):
        high, low = two_terms(table[t])
        chosen = counts[d, :, t].reshape(rows * samples, rows_dev).astype(jnp.bfloat16)
        part = matmul(chosen, high) + matmul(chosen, low)
        partials[:, t] = part.reshape(rows, samples, features)

    pool_copies = [
        remote(partials.at[peer], pools.at[r], pool_send.at[i], pool_recv.at[r], {"row": peer})
        for i, peer in enumerate(row_peers)
    ]
    for copy in pool_copies:
        copy.start()
    for copy in count_copies:
        copy.start()
    passed = [
        remote(counts.at[d], counts.at[d], count_pass.at[0], count_recv.at[d], {"depth": partner})
    ]
    passed[0].start()
    pools[r] = partials[r]

    dequant = (dense_q[...].astype(jnp.float32) - 128.0) / 64.0
    dense_vec = jnp.zeros((samples, features), jnp.float32)
    for i in range(bottom_w.shape[0]):
        dense_vec = dense_vec + dequant[:, i : i + 1] * bottom_w[i : i + 1, :]
    label_col = jnp.zeros((samples, 1), jnp.float32)
    sample_at = lax.broadcasted_iota(jnp.int32, (samples, 1), 0)
    for b in range(samples):
        label_col = jnp.where(sample_at == b, labels[b].astype(jnp.float32), label_col)
    diagonal = lax.broadcasted_iota(jnp.int32, (rows_dev, rows_dev), 0) == lax.broadcasted_iota(
        jnp.int32, (rows_dev, rows_dev), 1
    )
    for t in range(tables):
        state_cols[t] = jnp.sum(
            jnp.where(diagonal, accum[t : t + 1, :], 0.0), axis=1, keepdims=True
        )

    for peer in row_peers:
        remote(
            pools.at[peer], pools.at[peer], pool_send.at[0], pool_recv.at[peer], {"row": peer}
        ).wait_recv()

    bag_scale = float(bag_size) ** (-0.5)
    width_scale = float(features) ** (-0.5)
    vectors = [dense_vec] + [bag_scale * jnp.sum(pools[:, t], axis=0) for t in range(tables)]
    pair_at = {}
    for i in range(tables + 1):
        for k in range(i + 1, tables + 1):
            pair_at[i, k] = pair_at[k, i] = len(pair_at) // 2
    mixed = []
    for i in range(tables + 1):
        terms = [top_w[pair_at[i, k]] * vectors[k] for k in range(tables + 1) if k != i]
        mixed.append(functools.reduce(jnp.add, terms))
    joined = functools.reduce(jnp.add, [vectors[i] * mixed[i] for i in range(tables + 1)])
    logit = (0.5 * width_scale) * jnp.sum(joined, axis=1, keepdims=True)
    coeff = (1.0 / (1.0 + jnp.exp(-logit)) - label_col) * (bag_scale * width_scale)
    for t in range(tables):
        grads[d, r, t] = coeff * mixed[1 + t]

    grad_copies = []
    for i, peer in enumerate(row_peers):
        grad_copies.append(
            remote(
                grads.at[d, r], grads.at[d, r], grad_send.at[i], grad_recv.at[d, r], {"row": peer}
            )
        )

    def spread(n, row):
        made = [
            remote(
                grads.at[d, row],
                grads.at[d, row],
                grad_spread.at[n, i],
                grad_recv.at[d, row],
                {"depth": peer},
            )
            for i, peer in enumerate(depth_peers)
        ]
        made.append(pass_on(0, n, d, row))
        for copy in made:
            copy.start()
        return made

    def pass_on(m, n, depth, row):
        return remote(
            grads.at[depth, row],
            grads.at[depth, row],
            grad_pass.at[m, n],
            grad_recv.at[depth, row],
            {"depth": partner},
        )

    for copy in grad_copies:
        copy.start()
    grad_copies += spread(0, r)

    eye = lax.broadcasted_iota(jnp.int32, (samples, samples), 0) == lax.broadcasted_iota(
        jnp.int32, (samples, samples), 1
    )
    logits_out[...] = jnp.sum(jnp.where(eye, logit, 0.0), axis=0, keepdims=True)

    for n, peer in enumerate(row_peers):
        remote(
            grads.at[d, peer], grads.at[d, peer], grad_send.at[0], grad_recv.at[d, peer], {"row": peer}
        ).wait_recv()
        grad_copies += spread(n + 1, peer)

    for m, peer in enumerate(depth_peers):
        remote(
            counts.at[peer], counts.at[peer], count_send.at[0], count_recv.at[peer], {"depth": peer}
        ).wait_recv()
        copy = remote(
            counts.at[peer],
            counts.at[peer],
            count_pass.at[m + 1],
            count_recv.at[peer],
            {"depth": partner},
        )
        copy.start()
        passed.append(copy)

    for n, row in enumerate([r] + row_peers):
        for m, peer in enumerate(depth_peers):
            remote(
                grads.at[peer, row],
                grads.at[peer, row],
                grad_send.at[0],
                grad_recv.at[peer, row],
                {"depth": peer},
            ).wait_recv()
            copy = pass_on(m + 1, n, peer, row)
            copy.start()
            grad_copies.append(copy)

    for peer in partner_side:
        remote(
            counts.at[peer], counts.at[peer], count_send.at[0], count_recv.at[peer], {"depth": partner}
        ).wait_recv()
    batch = depths * rows * samples
    for t in range(tables):
        weights[t] = counts[:, :, t].reshape(batch, rows_dev).T.astype(jnp.bfloat16)

    for row in [r] + row_peers:
        for peer in partner_side:
            remote(
                grads.at[peer, row],
                grads.at[peer, row],
                grad_send.at[0],
                grad_recv.at[peer, row],
                {"depth": partner},
            ).wait_recv()

    for t in range(tables):
        high, low = two_terms(grads[:, :, t].reshape(batch, features))
        row_grad = matmul(weights[t], high) + matmul(weights[t], low)
        state = state_cols[t] + jnp.sum(row_grad * row_grad, axis=1, keepdims=True) / features
        new_table[t] = table[t] - row_grad * (LEARN_RATE / (jnp.sqrt(state) + EPSILON))
        new_accum[t : t + 1, :] = jnp.sum(jnp.where(diagonal, state, 0.0), axis=0, keepdims=True)

    for copy in code_copies + count_copies + passed + pool_copies + grad_copies:
        copy.wait_send()


def shards_small(table, accum, owner, local_row, lengths, dense_q, labels, bottom_w, top_w):
    tables, rows_dev, features = table.shape
    samples, bag_size = (owner.shape[0], owner.shape[2])
    rows = lax.axis_size("row")
    depths = lax.axis_size("depth")
    half = depths // 2
    f32 = jnp.float32
    dma = pltpu.SemaphoreType.DMA
    vmem = pl.BlockSpec(memory_space=pltpu.VMEM)
    smem = pl.BlockSpec(memory_space=pltpu.SMEM)
    block = (tables, samples, features)
    new_table, new_accum, logits = pl.pallas_call(
        step_kernel,
        out_shape=[
            jax.ShapeDtypeStruct(table.shape, f32),
            jax.ShapeDtypeStruct(accum.shape, f32),
            jax.ShapeDtypeStruct((1, samples), f32),
        ],
        in_specs=[vmem, vmem, vmem, vmem, vmem, vmem, smem, vmem, smem],
        out_specs=[vmem, vmem, vmem],
        scratch_shapes=[
            pltpu.VMEM((rows, tables // 2, samples, 2 * bag_size), jnp.int32),
            pltpu.VMEM((depths, rows, tables, samples, rows_dev), f32),
            pltpu.VMEM((rows,) + block, f32),
            pltpu.VMEM((rows,) + block, f32),
            pltpu.VMEM((depths, rows) + block, f32),
            pltpu.VMEM((tables, rows_dev, depths * rows * samples), jnp.bfloat16),
            pltpu.VMEM((tables, rows_dev, 1), f32),
            dma((rows - 1,)),
            dma((rows,)),
            dma((half - 1,)),
            dma((half,)),
            dma((depths,)),
            dma((rows - 1,)),
            dma((rows,)),
            dma((rows - 1,)),
            dma((rows, half - 1)),
            dma((half, rows)),
            dma((depths, rows)),
        ],
        compiler_params=pltpu.CompilerParams(
            collective_id=0, has_side_effects=True, vmem_limit_bytes=32 * 1024 * 1024
        ),
    )(
        table,
        accum,
        owner.reshape(samples, tables, bag_size),
        local_row,
        lengths,
        dense_q,
        labels,
        bottom_w,
        top_w,
    )
    return new_table, new_accum, logits.reshape(samples)


def by_size(table, *rest):
    tables, _, features = table.shape
    samples = rest[1].shape[0]
    devices = lax.axis_size("row") * lax.axis_size("depth")
    gathered = devices * samples * tables * features * 4
    if gathered <= 4 * 1024 * 1024:
        return shards_small(table, *rest)
    return shards_large(table, *rest)


def solution(mesh):
    in_specs = (
        P(None, "row", None),
        P(None, "row"),
        P(("row", "depth"), None, None, None),
        P(("row", "depth"), None, None),
        P(("row", "depth"), None),
        P(("row", "depth"), None),
        P(("row", "depth")),
        P(),
        P(),
    )
    out_specs = (P(None, "row", None), P(None, "row"), P(("row", "depth")))
    return jax.shard_map(by_size, mesh=mesh, in_specs=in_specs, out_specs=out_specs, check_vma=False)
```

```python
import functools

import jax
import jax.numpy as jnp
import numpy as np
from jax import lax
from jax.experimental import pallas as pl
from jax.experimental.pallas import tpu as pltpu
from jax.sharding import PartitionSpec as P

LEARN_RATE = 0.5
EPSILON = 1e-08


def pair_matrix(top_w, count):
    upper_i, upper_k = np.triu_indices(count, 1)
    matrix = jnp.zeros((count, count), jnp.float32)
    matrix = matrix.at[upper_i, upper_k].set(top_w)
    return matrix.at[upper_k, upper_i].set(top_w)


def adagrad(rows_now, state_now, gradient):
    state = state_now + jnp.mean(gradient * gradient, axis=1)
    return (rows_now - LEARN_RATE * gradient / (jnp.sqrt(state)[:, None] + EPSILON), state)


def shards_large(table, accum, owner, local_row, lengths, dense_q, labels, bottom_w, top_w):
    tables, rows_dev, features = table.shape
    samples, bag_size = (owner.shape[0], owner.shape[2])
    row_devices = lax.axis_size("row")
    slot_count = samples * tables * bag_size
    bag_count = samples * tables
    capacity = 2 * slot_count // row_devices
    row_span = tables * rows_dev
    owner_of = owner.reshape(slot_count)
    local_of = local_row.reshape(slot_count)
    slot_live = (
        lax.broadcasted_iota(jnp.int32, (samples, tables, bag_size), 2) < lengths[:, :, None]
    ).reshape(slot_count)
    slot_index = jnp.arange(slot_count, dtype=jnp.int32)
    bag_of = slot_index // bag_size
    table_of = bag_of % tables
    entry_codes = jnp.where(slot_live, bag_of * row_span + table_of * rows_dev + local_of, -1)
    owner_hits = (owner_of[:, None] == jnp.arange(row_devices, dtype=jnp.int32)[None, :]).astype(
        jnp.int32
    )
    before = jnp.cumsum(owner_hits, axis=0) - owner_hits
    position = jnp.sum(before * owner_hits, axis=1)
    outgoing = (
        jnp.full((row_devices * capacity,), -1, jnp.int32)
        .at[owner_of * capacity + position]
        .set(entry_codes)
    )
    received = lax.all_to_all(
        outgoing.reshape(row_devices, capacity), "row", split_axis=0, concat_axis=0, tiled=True
    )
    is_live = received >= 0
    flat_rows = jnp.where(is_live, received % row_span, 0)
    bag_at = jnp.where(is_live, received // row_span, -1)
    flat_table = table.reshape(row_span, features)
    picked = flat_table[flat_rows]
    choose = (bag_at[:, None, :] == jnp.arange(bag_count, dtype=jnp.int32)[None, :, None]).astype(
        jnp.float32
    )
    partial_pool = jnp.einsum("sbc,scw->sbw", choose, picked, precision=lax.Precision.HIGHEST)
    returned = lax.all_to_all(partial_pool, "row", split_axis=0, concat_axis=0, tiled=True)
    pooled = jnp.sum(returned, axis=0).reshape(samples, tables, features)
    dequant = (dense_q.astype(jnp.float32) - 128.0) / 64.0
    dense_vec = jnp.dot(dequant, bottom_w, precision=lax.Precision.HIGHEST)
    bag_scale = float(bag_size) ** (-0.5)
    width_scale = float(features) ** (-0.5)
    vectors = jnp.concatenate([dense_vec[:, None, :], bag_scale * pooled], axis=1)
    dots = width_scale * jnp.einsum(
        "biw,bkw->bik", vectors, vectors, precision=lax.Precision.HIGHEST
    )
    matrix = pair_matrix(top_w, tables + 1)
    logits = 0.5 * jnp.sum(dots * matrix[None, :, :], axis=(1, 2))
    loss_coeff = (jax.nn.sigmoid(logits) - labels.astype(jnp.float32)) * bag_scale * width_scale
    mixed = jnp.einsum("ti,biw->btw", matrix[1:, :], vectors, precision=lax.Precision.HIGHEST)
    pooled_grad = (loss_coeff[:, None, None] * mixed).reshape(1, bag_count, features)
    piece = lax.all_gather(pooled_grad, "row", axis=0, tiled=True)
    piece_sources = piece.shape[0]
    piece_live = received >= 0
    piece_bags = jnp.where(piece_live, received // row_span, 0)
    source_at = jnp.arange(piece_sources, dtype=jnp.int32)[:, None]
    slot_grads = piece[source_at, piece_bags] * piece_live[:, :, None].astype(jnp.float32)
    row_grad = (
        jnp.zeros((row_span, features), jnp.float32)
        .at[flat_rows.reshape(-1)]
        .add(slot_grads.reshape(-1, features))
    )
    flat_accum = accum.reshape(row_span)
    summed = lax.psum(row_grad, "depth")
    new_rows, new_state = adagrad(flat_table, flat_accum, summed)
    return (
        new_rows.reshape(tables, rows_dev, features),
        new_state.reshape(tables, rows_dev),
        logits,
    )


def remote(src, dst, send_sem, recv_sem, device):
    return pltpu.make_async_remote_copy(
        src_ref=src,
        dst_ref=dst,
        send_sem=send_sem,
        recv_sem=recv_sem,
        device_id=device,
        device_id_type=pl.DeviceIdType.MESH,
    )


def two_terms(value):
    high = value.astype(jnp.bfloat16)
    return high, (value - high.astype(jnp.float32)).astype(jnp.bfloat16)


def matmul(a, b):
    return lax.dot_general(a, b, (((1,), (0,)), ((), ())), preferred_element_type=jnp.float32)


def step_kernel(
    table_in,
    accum_in,
    owner_in,
    local_in,
    lengths_in,
    dense_in,
    labels_in,
    bottom_in,
    top_in,
    new_table,
    new_accum,
    logits_out,
    table,
    accum,
    owner,
    local_row,
    lengths,
    dense_q,
    labels,
    bottom_w,
    top_w,
    table_high,
    table_low,
    fetch,
    codes,
    counts,
    partials,
    pools,
    grads,
    weights,
    state_cols,
    code_send,
    code_recv,
    count_send,
    count_pass,
    count_recv,
    pool_send,
    pool_recv,
    grad_send,
    grad_spread,
    grad_pass,
    grad_recv,
):
    rows = codes.shape[0]
    depths = counts.shape[0]
    half = depths // 2
    tables, rows_dev, features = table.shape
    samples, _, bag_size = owner.shape
    r = lax.axis_index("row")
    d = lax.axis_index("depth")
    partner = d + 1 - 2 * lax.rem(d, 2)
    row_peers = [lax.rem(r + k, rows) for k in range(1, rows)]
    depth_peers = [lax.rem(d + 2 * k, depths) for k in range(1, half)]
    partner_side = [partner] + [lax.rem(partner + 2 * k, depths) for k in range(1, half)]

    barrier = pltpu.get_barrier_semaphore()
    for peer in row_peers:
        pl.semaphore_signal(
            barrier, inc=1, device_id={"row": peer}, device_id_type=pl.DeviceIdType.MESH
        )
    for peer in depth_peers + [partner]:
        pl.semaphore_signal(
            barrier, inc=1, device_id={"depth": peer}, device_id_type=pl.DeviceIdType.MESH
        )

    fetches = [
        pltpu.make_async_copy(source, target, fetch.at[i])
        for i, (source, target) in enumerate(
            [
                (owner_in, owner),
                (local_in, local_row),
                (lengths_in, lengths),
                (table_in, table),
                (accum_in, accum),
                (dense_in, dense_q),
                (labels_in, labels),
                (bottom_in, bottom_w),
                (top_in, top_w),
            ]
        )
    ]
    for copy in fetches:
        copy.start()
    eye = lax.broadcasted_iota(jnp.int32, (samples, samples), 0) == lax.broadcasted_iota(
        jnp.int32, (samples, samples), 1
    )
    for copy in fetches[:3]:
        copy.wait()

    slot_at = lax.broadcasted_iota(jnp.int32, (samples, bag_size), 1).astype(jnp.float32)
    lengths_f = lengths[...].astype(jnp.float32)
    mine = []
    for t in range(tables):
        live = slot_at < jnp.sum(jnp.where(eye, lengths_f[t : t + 1, :], 0.0), axis=1, keepdims=True)
        mine.append(jnp.where(live, owner[:, t, :] * rows_dev + local_row[:, t, :], -1))
    for p in range(tables // 2):
        codes[r, p] = jnp.concatenate([mine[2 * p], mine[2 * p + 1]], axis=1)

    pl.semaphore_wait(barrier, rows - 1 + half)

    code_copies = [
        remote(codes.at[r], codes.at[r], code_send.at[i], code_recv.at[r], {"row": peer})
        for i, peer in enumerate(row_peers)
    ]
    for copy in code_copies:
        copy.start()

    row_at = lax.broadcasted_iota(jnp.int32, (samples, rows_dev), 1)

    def count(source):
        def pair(p, carry):
            relative = codes[source, p] - r * rows_dev
            for side in range(2):
                total = jnp.zeros((samples, rows_dev), jnp.float32)
                for j in range(bag_size):
                    at = side * bag_size + j
                    total = total + jnp.where(relative[:, at : at + 1] == row_at, 1.0, 0.0)
                counts[d, source, 2 * p + side] = total
            return carry

        lax.fori_loop(0, tables // 2, pair, 0)

    def pool_copy(k, source):
        return remote(
            partials.at[source], pools.at[r], pool_send.at[k], pool_recv.at[r], {"row": source}
        )

    def pool(source, target):
        for t in range(tables):
            chosen = counts[d, source, t].astype(jnp.bfloat16)
            target[source, t] = matmul(chosen, table_high[t]) + matmul(chosen, table_low[t])

    count(r)
    for copy in fetches[3:]:
        copy.wait()
    for t in range(tables):
        table_high[t], table_low[t] = two_terms(table[t])

    def count_peer(k, carry):
        source = lax.rem(r + k, rows)
        remote(
            codes.at[source], codes.at[source], code_send.at[0], code_recv.at[source], {"row": source}
        ).wait_recv()
        count(source)
        pool(source, partials)
        pool_copy(k - 1, source).start()
        return carry

    lax.fori_loop(1, rows, count_peer, 0)

    count_copies = [
        remote(counts.at[d], counts.at[d], count_send.at[i], count_recv.at[d], {"depth": peer})
        for i, peer in enumerate(depth_peers)
    ]

    pool_copies = [pool_copy(i, peer) for i, peer in enumerate(row_peers)]
    for copy in count_copies:
        copy.start()
    passed = [
        remote(counts.at[d], counts.at[d], count_pass.at[0], count_recv.at[d], {"depth": partner})
    ]
    passed[0].start()
    pool(r, pools)

    dequant = (dense_q[...].astype(jnp.float32) - 128.0) / 64.0
    dense_vec = jnp.zeros((samples, features), jnp.float32)
    for i in range(bottom_w.shape[0]):
        dense_vec = dense_vec + dequant[:, i : i + 1] * bottom_w[i : i + 1, :]
    label_col = jnp.zeros((samples, 1), jnp.float32)
    sample_at = lax.broadcasted_iota(jnp.int32, (samples, 1), 0)
    for b in range(samples):
        label_col = jnp.where(sample_at == b, labels[b].astype(jnp.float32), label_col)
    diagonal = lax.broadcasted_iota(jnp.int32, (rows_dev, rows_dev), 0) == lax.broadcasted_iota(
        jnp.int32, (rows_dev, rows_dev), 1
    )
    for t in range(tables):
        state_cols[t] = jnp.sum(
            jnp.where(diagonal, accum[t : t + 1, :], 0.0), axis=1, keepdims=True
        )

    for peer in row_peers:
        remote(
            pools.at[peer], pools.at[peer], pool_send.at[0], pool_recv.at[peer], {"row": peer}
        ).wait_recv()

    bag_scale = float(bag_size) ** (-0.5)
    width_scale = float(features) ** (-0.5)
    vectors = [dense_vec] + [bag_scale * jnp.sum(pools[:, t], axis=0) for t in range(tables)]
    pair_at = {}
    for i in range(tables + 1):
        for k in range(i + 1, tables + 1):
            pair_at[i, k] = pair_at[k, i] = len(pair_at) // 2
    mixed = []
    for i in range(tables + 1):
        terms = [top_w[pair_at[i, k]] * vectors[k] for k in range(tables + 1) if k != i]
        mixed.append(functools.reduce(jnp.add, terms))
    joined = functools.reduce(jnp.add, [vectors[i] * mixed[i] for i in range(tables + 1)])
    logit = (0.5 * width_scale) * jnp.sum(joined, axis=1, keepdims=True)
    coeff = (1.0 / (1.0 + jnp.exp(-logit)) - label_col) * (bag_scale * width_scale)
    for t in range(tables):
        grads[d, r, t] = coeff * mixed[1 + t]

    grad_copies = []
    for i, peer in enumerate(row_peers):
        grad_copies.append(
            remote(
                grads.at[d, r], grads.at[d, r], grad_send.at[i], grad_recv.at[d, r], {"row": peer}
            )
        )

    def spread(n, row):
        made = [
            remote(
                grads.at[d, row],
                grads.at[d, row],
                grad_spread.at[n, i],
                grad_recv.at[d, row],
                {"depth": peer},
            )
            for i, peer in enumerate(depth_peers)
        ]
        made.append(pass_on(0, n, d, row))
        for copy in made:
            copy.start()
        return made

    def pass_on(m, n, depth, row):
        return remote(
            grads.at[depth, row],
            grads.at[depth, row],
            grad_pass.at[m, n],
            grad_recv.at[depth, row],
            {"depth": partner},
        )

    for copy in grad_copies:
        copy.start()
    grad_copies += spread(0, r)

    logits_out[...] = jnp.sum(jnp.where(eye, logit, 0.0), axis=0, keepdims=True)

    for n, peer in enumerate(row_peers):
        remote(
            grads.at[d, peer], grads.at[d, peer], grad_send.at[0], grad_recv.at[d, peer], {"row": peer}
        ).wait_recv()
        grad_copies += spread(n + 1, peer)

    for m, peer in enumerate(depth_peers):
        remote(
            counts.at[peer], counts.at[peer], count_send.at[0], count_recv.at[peer], {"depth": peer}
        ).wait_recv()
        copy = remote(
            counts.at[peer],
            counts.at[peer],
            count_pass.at[m + 1],
            count_recv.at[peer],
            {"depth": partner},
        )
        copy.start()
        passed.append(copy)

    for n, row in enumerate([r] + row_peers):
        for m, peer in enumerate(depth_peers):
            remote(
                grads.at[peer, row],
                grads.at[peer, row],
                grad_send.at[0],
                grad_recv.at[peer, row],
                {"depth": peer},
            ).wait_recv()
            copy = pass_on(m + 1, n, peer, row)
            copy.start()
            grad_copies.append(copy)

    for peer in partner_side:
        remote(
            counts.at[peer], counts.at[peer], count_send.at[0], count_recv.at[peer], {"depth": partner}
        ).wait_recv()
    batch = depths * rows * samples
    for t in range(tables):
        weights[t] = counts[:, :, t].reshape(batch, rows_dev).T.astype(jnp.bfloat16)

    for row in [r] + row_peers:
        for peer in partner_side:
            remote(
                grads.at[peer, row],
                grads.at[peer, row],
                grad_send.at[0],
                grad_recv.at[peer, row],
                {"depth": partner},
            ).wait_recv()

    for t in range(tables):
        high, low = two_terms(grads[:, :, t].reshape(batch, features))
        row_grad = matmul(weights[t], high) + matmul(weights[t], low)
        state = state_cols[t] + jnp.sum(row_grad * row_grad, axis=1, keepdims=True) / features
        new_table[t] = table[t] - row_grad * (LEARN_RATE / (jnp.sqrt(state) + EPSILON))
        new_accum[t : t + 1, :] = jnp.sum(jnp.where(diagonal, state, 0.0), axis=0, keepdims=True)

    for copy in code_copies + count_copies + passed + pool_copies + grad_copies:
        copy.wait_send()


def shards_small(table, accum, owner, local_row, lengths, dense_q, labels, bottom_w, top_w):
    tables, rows_dev, features = table.shape
    samples, bag_size = (owner.shape[0], owner.shape[2])
    rows = lax.axis_size("row")
    depths = lax.axis_size("depth")
    half = depths // 2
    f32 = jnp.float32
    dma = pltpu.SemaphoreType.DMA
    vmem = pl.BlockSpec(memory_space=pltpu.VMEM)
    hbm = pl.BlockSpec(memory_space=pltpu.HBM)
    i32 = jnp.int32
    block = (tables, samples, features)
    new_table, new_accum, logits = pl.pallas_call(
        step_kernel,
        out_shape=[
            jax.ShapeDtypeStruct(table.shape, f32),
            jax.ShapeDtypeStruct(accum.shape, f32),
            jax.ShapeDtypeStruct((1, samples), f32),
        ],
        in_specs=[hbm] * 9,
        out_specs=[vmem, vmem, vmem],
        scratch_shapes=[
            pltpu.VMEM(table.shape, f32),
            pltpu.VMEM(accum.shape, f32),
            pltpu.VMEM((samples, tables, bag_size), i32),
            pltpu.VMEM(local_row.shape, i32),
            pltpu.VMEM((tables, samples), i32),
            pltpu.VMEM(dense_q.shape, i32),
            pltpu.SMEM(labels.shape, i32),
            pltpu.VMEM(bottom_w.shape, f32),
            pltpu.SMEM(top_w.shape, f32),
            pltpu.VMEM(table.shape, jnp.bfloat16),
            pltpu.VMEM(table.shape, jnp.bfloat16),
            dma((9,)),
            pltpu.VMEM((rows, tables // 2, samples, 2 * bag_size), jnp.int32),
            pltpu.VMEM((depths, rows, tables, samples, rows_dev), f32),
            pltpu.VMEM((rows,) + block, f32),
            pltpu.VMEM((rows,) + block, f32),
            pltpu.VMEM((depths, rows) + block, f32),
            pltpu.VMEM((tables, rows_dev, depths * rows * samples), jnp.bfloat16),
            pltpu.VMEM((tables, rows_dev, 1), f32),
            dma((rows - 1,)),
            dma((rows,)),
            dma((half - 1,)),
            dma((half,)),
            dma((depths,)),
            dma((rows - 1,)),
            dma((rows,)),
            dma((rows - 1,)),
            dma((rows, half - 1)),
            dma((half, rows)),
            dma((depths, rows)),
        ],
        compiler_params=pltpu.CompilerParams(
            collective_id=0, has_side_effects=True, vmem_limit_bytes=63 * 1024 * 1024
        ),
    )(
        table,
        accum,
        owner.reshape(samples, tables, bag_size),
        local_row,
        lengths.T,
        dense_q,
        labels,
        bottom_w,
        top_w,
    )
    return new_table, new_accum, logits.reshape(samples)


def by_size(table, *rest):
    tables, _, features = table.shape
    samples = rest[1].shape[0]
    devices = lax.axis_size("row") * lax.axis_size("depth")
    gathered = devices * samples * tables * features * 4
    if gathered <= 4 * 1024 * 1024:
        return shards_small(table, *rest)
    return shards_large(table, *rest)


def solution(mesh):
    in_specs = (
        P(None, "row", None),
        P(None, "row"),
        P(("row", "depth"), None, None, None),
        P(("row", "depth"), None, None),
        P(("row", "depth"), None),
        P(("row", "depth"), None),
        P(("row", "depth")),
        P(),
        P(),
    )
    out_specs = (P(None, "row", None), P(None, "row"), P(("row", "depth")))
    return jax.shard_map(by_size, mesh=mesh, in_specs=in_specs, out_specs=out_specs, check_vma=False)
```

```python
import functools

import jax
import jax.numpy as jnp
import numpy as np
from jax import lax
from jax.experimental import pallas as pl
from jax.experimental.pallas import tpu as pltpu
from jax.sharding import PartitionSpec as P

LEARN_RATE = 0.5
EPSILON = 1e-08


def pair_matrix(top_w, count):
    upper_i, upper_k = np.triu_indices(count, 1)
    matrix = jnp.zeros((count, count), jnp.float32)
    matrix = matrix.at[upper_i, upper_k].set(top_w)
    return matrix.at[upper_k, upper_i].set(top_w)


def adagrad(rows_now, state_now, gradient):
    state = state_now + jnp.mean(gradient * gradient, axis=1)
    return (rows_now - LEARN_RATE * gradient / (jnp.sqrt(state)[:, None] + EPSILON), state)


def shards_large(table, accum, owner, local_row, lengths, dense_q, labels, bottom_w, top_w):
    tables, rows_dev, features = table.shape
    samples, bag_size = (owner.shape[0], owner.shape[2])
    row_devices = lax.axis_size("row")
    slot_count = samples * tables * bag_size
    bag_count = samples * tables
    capacity = 2 * slot_count // row_devices
    row_span = tables * rows_dev
    owner_of = owner.reshape(slot_count)
    local_of = local_row.reshape(slot_count)
    slot_live = (
        lax.broadcasted_iota(jnp.int32, (samples, tables, bag_size), 2) < lengths[:, :, None]
    ).reshape(slot_count)
    slot_index = jnp.arange(slot_count, dtype=jnp.int32)
    bag_of = slot_index // bag_size
    table_of = bag_of % tables
    entry_codes = jnp.where(slot_live, bag_of * row_span + table_of * rows_dev + local_of, -1)
    owner_hits = (owner_of[:, None] == jnp.arange(row_devices, dtype=jnp.int32)[None, :]).astype(
        jnp.int32
    )
    before = jnp.cumsum(owner_hits, axis=0) - owner_hits
    position = jnp.sum(before * owner_hits, axis=1)
    outgoing = (
        jnp.full((row_devices * capacity,), -1, jnp.int32)
        .at[owner_of * capacity + position]
        .set(entry_codes)
    )
    received = lax.all_to_all(
        outgoing.reshape(row_devices, capacity), "row", split_axis=0, concat_axis=0, tiled=True
    )
    is_live = received >= 0
    flat_rows = jnp.where(is_live, received % row_span, 0)
    bag_at = jnp.where(is_live, received // row_span, -1)
    flat_table = table.reshape(row_span, features)
    picked = flat_table[flat_rows]
    choose = (bag_at[:, None, :] == jnp.arange(bag_count, dtype=jnp.int32)[None, :, None]).astype(
        jnp.float32
    )
    partial_pool = jnp.einsum("sbc,scw->sbw", choose, picked, precision=lax.Precision.HIGHEST)
    returned = lax.all_to_all(partial_pool, "row", split_axis=0, concat_axis=0, tiled=True)
    pooled = jnp.sum(returned, axis=0).reshape(samples, tables, features)
    dequant = (dense_q.astype(jnp.float32) - 128.0) / 64.0
    dense_vec = jnp.dot(dequant, bottom_w, precision=lax.Precision.HIGHEST)
    bag_scale = float(bag_size) ** (-0.5)
    width_scale = float(features) ** (-0.5)
    vectors = jnp.concatenate([dense_vec[:, None, :], bag_scale * pooled], axis=1)
    dots = width_scale * jnp.einsum(
        "biw,bkw->bik", vectors, vectors, precision=lax.Precision.HIGHEST
    )
    matrix = pair_matrix(top_w, tables + 1)
    logits = 0.5 * jnp.sum(dots * matrix[None, :, :], axis=(1, 2))
    loss_coeff = (jax.nn.sigmoid(logits) - labels.astype(jnp.float32)) * bag_scale * width_scale
    mixed = jnp.einsum("ti,biw->btw", matrix[1:, :], vectors, precision=lax.Precision.HIGHEST)
    pooled_grad = (loss_coeff[:, None, None] * mixed).reshape(1, bag_count, features)
    piece = lax.all_gather(pooled_grad, "row", axis=0, tiled=True)
    piece_sources = piece.shape[0]
    piece_live = received >= 0
    piece_bags = jnp.where(piece_live, received // row_span, 0)
    source_at = jnp.arange(piece_sources, dtype=jnp.int32)[:, None]
    slot_grads = piece[source_at, piece_bags] * piece_live[:, :, None].astype(jnp.float32)
    row_grad = (
        jnp.zeros((row_span, features), jnp.float32)
        .at[flat_rows.reshape(-1)]
        .add(slot_grads.reshape(-1, features))
    )
    flat_accum = accum.reshape(row_span)
    summed = lax.psum(row_grad, "depth")
    new_rows, new_state = adagrad(flat_table, flat_accum, summed)
    return (
        new_rows.reshape(tables, rows_dev, features),
        new_state.reshape(tables, rows_dev),
        logits,
    )


def remote(src, dst, send_sem, recv_sem, device):
    return pltpu.make_async_remote_copy(
        src_ref=src,
        dst_ref=dst,
        send_sem=send_sem,
        recv_sem=recv_sem,
        device_id=device,
        device_id_type=pl.DeviceIdType.MESH,
    )


def two_terms(value):
    high = value.astype(jnp.bfloat16)
    return high, (value - high.astype(jnp.float32)).astype(jnp.bfloat16)


def matmul(a, b):
    return lax.dot_general(a, b, (((1,), (0,)), ((), ())), preferred_element_type=jnp.float32)


def step_kernel(
    table_in,
    owner_in,
    local_in,
    lengths_in,
    dense_in,
    labels_in,
    bottom_in,
    top_in,
    row_grad_out,
    logits_out,
    table,
    owner,
    local_row,
    lengths,
    dense_q,
    labels,
    bottom_w,
    top_w,
    table_high,
    table_low,
    fetch,
    codes,
    counts,
    partials,
    pools,
    grads,
    weights,
    row_grad,
    store,
    code_send,
    code_recv,
    count_send,
    count_pass,
    count_recv,
    pool_send,
    pool_recv,
    grad_send,
    grad_spread,
    grad_pass,
    grad_recv,
):
    rows = codes.shape[0]
    depths = counts.shape[0]
    half = depths // 2
    tables, rows_dev, features = table.shape
    samples, _, bag_size = owner.shape
    r = lax.axis_index("row")
    d = lax.axis_index("depth")
    partner = d + 1 - 2 * lax.rem(d, 2)
    row_peers = [lax.rem(r + k, rows) for k in range(1, rows)]
    depth_peers = [lax.rem(d + 2 * k, depths) for k in range(1, half)]
    partner_side = [partner] + [lax.rem(partner + 2 * k, depths) for k in range(1, half)]

    barrier = pltpu.get_barrier_semaphore()
    for peer in row_peers:
        pl.semaphore_signal(
            barrier, inc=1, device_id={"row": peer}, device_id_type=pl.DeviceIdType.MESH
        )
    for peer in depth_peers + [partner]:
        pl.semaphore_signal(
            barrier, inc=1, device_id={"depth": peer}, device_id_type=pl.DeviceIdType.MESH
        )

    fetches = [
        pltpu.make_async_copy(source, target, fetch.at[i])
        for i, (source, target) in enumerate(
            [
                (owner_in, owner),
                (local_in, local_row),
                (lengths_in, lengths),
                (table_in, table),
                (dense_in, dense_q),
                (labels_in, labels),
                (bottom_in, bottom_w),
                (top_in, top_w),
            ]
        )
    ]
    for copy in fetches:
        copy.start()
    eye = lax.broadcasted_iota(jnp.int32, (samples, samples), 0) == lax.broadcasted_iota(
        jnp.int32, (samples, samples), 1
    )
    for copy in fetches[:3]:
        copy.wait()

    slot_at = lax.broadcasted_iota(jnp.int32, (samples, bag_size), 1).astype(jnp.float32)
    lengths_f = lengths[...].astype(jnp.float32)
    mine = []
    for t in range(tables):
        live = slot_at < jnp.sum(jnp.where(eye, lengths_f[t : t + 1, :], 0.0), axis=1, keepdims=True)
        mine.append(jnp.where(live, owner[:, t, :] * rows_dev + local_row[:, t, :], -1))
    for p in range(tables // 2):
        codes[r, p] = jnp.concatenate([mine[2 * p], mine[2 * p + 1]], axis=1)

    row_at = lax.broadcasted_iota(jnp.int32, (samples, rows_dev), 1)

    def count(source):
        def pair(p, carry):
            relative = codes[source, p] - r * rows_dev
            for side in range(2):
                total = jnp.zeros((samples, rows_dev), jnp.float32)
                for j in range(bag_size):
                    at = side * bag_size + j
                    total = total + jnp.where(relative[:, at : at + 1] == row_at, 1.0, 0.0)
                counts[d, source, 2 * p + side] = total
            return carry

        lax.fori_loop(0, tables // 2, pair, 0)

    def pool_copy(k, source):
        return remote(
            partials.at[source], pools.at[r], pool_send.at[k], pool_recv.at[r], {"row": source}
        )

    def pool(source, target):
        for t in range(tables):
            chosen = counts[d, source, t].astype(jnp.bfloat16)
            target[source, t] = matmul(chosen, table_high[t]) + matmul(chosen, table_low[t])

    count(r)
    for copy in fetches[3:]:
        copy.wait()
    for t in range(tables):
        table_high[t], table_low[t] = two_terms(table[t])

    pl.semaphore_wait(barrier, rows - 1 + half)

    code_copies = [
        remote(codes.at[r], codes.at[r], code_send.at[i], code_recv.at[r], {"row": peer})
        for i, peer in enumerate(row_peers)
    ]
    for copy in code_copies:
        copy.start()

    def count_peer(k, carry):
        source = lax.rem(r + k, rows)
        remote(
            codes.at[source], codes.at[source], code_send.at[0], code_recv.at[source], {"row": source}
        ).wait_recv()
        count(source)
        pool(source, partials)
        pool_copy(k - 1, source).start()
        return carry

    lax.fori_loop(1, rows, count_peer, 0)

    count_copies = [
        remote(counts.at[d], counts.at[d], count_send.at[i], count_recv.at[d], {"depth": peer})
        for i, peer in enumerate(depth_peers)
    ]

    pool_copies = [pool_copy(i, peer) for i, peer in enumerate(row_peers)]
    for copy in count_copies:
        copy.start()
    passed = [
        remote(counts.at[d], counts.at[d], count_pass.at[0], count_recv.at[d], {"depth": partner})
    ]
    passed[0].start()
    pool(r, pools)

    dequant = (dense_q[...].astype(jnp.float32) - 128.0) / 64.0
    dense_vec = jnp.zeros((samples, features), jnp.float32)
    for i in range(bottom_w.shape[0]):
        dense_vec = dense_vec + dequant[:, i : i + 1] * bottom_w[i : i + 1, :]
    label_col = jnp.zeros((samples, 1), jnp.float32)
    sample_at = lax.broadcasted_iota(jnp.int32, (samples, 1), 0)
    for b in range(samples):
        label_col = jnp.where(sample_at == b, labels[b].astype(jnp.float32), label_col)
    for peer in row_peers:
        remote(
            pools.at[peer], pools.at[peer], pool_send.at[0], pool_recv.at[peer], {"row": peer}
        ).wait_recv()

    bag_scale = float(bag_size) ** (-0.5)
    width_scale = float(features) ** (-0.5)
    vectors = [dense_vec] + [bag_scale * jnp.sum(pools[:, t], axis=0) for t in range(tables)]
    pair_at = {}
    for i in range(tables + 1):
        for k in range(i + 1, tables + 1):
            pair_at[i, k] = pair_at[k, i] = len(pair_at) // 2
    mixed = []
    for i in range(tables + 1):
        terms = [top_w[pair_at[i, k]] * vectors[k] for k in range(tables + 1) if k != i]
        mixed.append(functools.reduce(jnp.add, terms))
    joined = functools.reduce(jnp.add, [vectors[i] * mixed[i] for i in range(tables + 1)])
    logit = (0.5 * width_scale) * jnp.sum(joined, axis=1, keepdims=True)
    coeff = (1.0 / (1.0 + jnp.exp(-logit)) - label_col) * (bag_scale * width_scale)
    for t in range(tables):
        grads[d, r, t] = coeff * mixed[1 + t]

    grad_copies = []
    for i, peer in enumerate(row_peers):
        grad_copies.append(
            remote(
                grads.at[d, r], grads.at[d, r], grad_send.at[i], grad_recv.at[d, r], {"row": peer}
            )
        )

    def spread(n, row):
        made = [
            remote(
                grads.at[d, row],
                grads.at[d, row],
                grad_spread.at[n, i],
                grad_recv.at[d, row],
                {"depth": peer},
            )
            for i, peer in enumerate(depth_peers)
        ]
        made.append(pass_on(0, n, d, row))
        for copy in made:
            copy.start()
        return made

    def pass_on(m, n, depth, row):
        return remote(
            grads.at[depth, row],
            grads.at[depth, row],
            grad_pass.at[m, n],
            grad_recv.at[depth, row],
            {"depth": partner},
        )

    for copy in grad_copies:
        copy.start()
    grad_copies += spread(0, r)

    logits_out[...] = jnp.sum(jnp.where(eye, logit, 0.0), axis=0, keepdims=True)

    for n, peer in enumerate(row_peers):
        remote(
            grads.at[d, peer], grads.at[d, peer], grad_send.at[0], grad_recv.at[d, peer], {"row": peer}
        ).wait_recv()
        grad_copies += spread(n + 1, peer)

    for m, peer in enumerate(depth_peers):
        remote(
            counts.at[peer], counts.at[peer], count_send.at[0], count_recv.at[peer], {"depth": peer}
        ).wait_recv()
        copy = remote(
            counts.at[peer],
            counts.at[peer],
            count_pass.at[m + 1],
            count_recv.at[peer],
            {"depth": partner},
        )
        copy.start()
        passed.append(copy)

    for n, row in enumerate([r] + row_peers):
        for m, peer in enumerate(depth_peers):
            remote(
                grads.at[peer, row],
                grads.at[peer, row],
                grad_send.at[0],
                grad_recv.at[peer, row],
                {"depth": peer},
            ).wait_recv()
            copy = pass_on(m + 1, n, peer, row)
            copy.start()
            grad_copies.append(copy)

    for peer in partner_side:
        remote(
            counts.at[peer], counts.at[peer], count_send.at[0], count_recv.at[peer], {"depth": partner}
        ).wait_recv()
    batch = depths * rows * samples
    for t in range(tables):
        weights[t] = counts[:, :, t].reshape(batch, rows_dev).T.astype(jnp.bfloat16)

    for row in [r] + row_peers:
        for peer in partner_side:
            remote(
                grads.at[peer, row],
                grads.at[peer, row],
                grad_send.at[0],
                grad_recv.at[peer, row],
                {"depth": partner},
            ).wait_recv()

    for t in range(tables):
        high, low = two_terms(grads[:, :, t].reshape(batch, features))
        row_grad[t] = matmul(weights[t], high) + matmul(weights[t], low)
        pltpu.make_async_copy(row_grad.at[t], row_grad_out.at[t], store.at[t]).start()

    for t in range(tables):
        pltpu.make_async_copy(row_grad.at[t], row_grad_out.at[t], store.at[t]).wait()
    for copy in code_copies + count_copies + passed + pool_copies + grad_copies:
        copy.wait_send()


def update_kernel(
    grad_in,
    table_in,
    accum_in,
    logits_in,
    new_table,
    new_accum,
    logits_out,
    grad,
    table,
    accum,
    result,
    state_rows,
    fetch,
    store,
):
    tables, rows_dev, features = table.shape
    first = [
        pltpu.make_async_copy(accum_in, accum, fetch.at[2 * tables]),
        pltpu.make_async_copy(logits_in, logits_out, fetch.at[2 * tables + 1]),
    ]
    blocks = [
        (
            pltpu.make_async_copy(grad_in.at[t], grad.at[t], fetch.at[2 * t]),
            pltpu.make_async_copy(table_in.at[t], table.at[t], fetch.at[2 * t + 1]),
        )
        for t in range(tables)
    ]
    stores = [
        pltpu.make_async_copy(result.at[t], new_table.at[t], store.at[t]) for t in range(tables)
    ]
    stores.append(pltpu.make_async_copy(state_rows, new_accum, store.at[tables]))
    for copy in first:
        copy.start()
    for pair in blocks:
        for copy in pair:
            copy.start()
    diagonal = lax.broadcasted_iota(jnp.int32, (rows_dev, rows_dev), 0) == lax.broadcasted_iota(
        jnp.int32, (rows_dev, rows_dev), 1
    )
    first[0].wait()
    before = [
        jnp.sum(jnp.where(diagonal, accum[t : t + 1, :], 0.0), axis=1, keepdims=True)
        for t in range(tables)
    ]
    for t in range(tables):
        for copy in blocks[t]:
            copy.wait()
        row_grad = grad[t]
        state = before[t] + jnp.sum(row_grad * row_grad, axis=1, keepdims=True) / features
        result[t] = table[t] - row_grad * (LEARN_RATE / (jnp.sqrt(state) + EPSILON))
        stores[t].start()
        state_rows[t : t + 1, :] = jnp.sum(
            jnp.where(diagonal, state, 0.0), axis=0, keepdims=True
        )
    stores[tables].start()
    first[1].wait()
    for copy in stores:
        copy.wait()


def shards_small(table, accum, owner, local_row, lengths, dense_q, labels, bottom_w, top_w):
    tables, rows_dev, features = table.shape
    samples, bag_size = (owner.shape[0], owner.shape[2])
    rows = lax.axis_size("row")
    depths = lax.axis_size("depth")
    half = depths // 2
    f32 = jnp.float32
    dma = pltpu.SemaphoreType.DMA
    vmem = pl.BlockSpec(memory_space=pltpu.VMEM)
    hbm = pl.BlockSpec(memory_space=pltpu.HBM)
    i32 = jnp.int32
    block = (tables, samples, features)
    params = dict(has_side_effects=True, vmem_limit_bytes=63 * 1024 * 1024)
    row_grad, logits = pl.pallas_call(
        step_kernel,
        out_shape=[
            jax.ShapeDtypeStruct(table.shape, f32),
            jax.ShapeDtypeStruct((1, samples), f32),
        ],
        in_specs=[hbm] * 8,
        out_specs=[hbm, vmem],
        scratch_shapes=[
            pltpu.VMEM(table.shape, f32),
            pltpu.VMEM((samples, tables, bag_size), i32),
            pltpu.VMEM(local_row.shape, i32),
            pltpu.VMEM((tables, samples), i32),
            pltpu.VMEM(dense_q.shape, i32),
            pltpu.SMEM(labels.shape, i32),
            pltpu.VMEM(bottom_w.shape, f32),
            pltpu.SMEM(top_w.shape, f32),
            pltpu.VMEM(table.shape, jnp.bfloat16),
            pltpu.VMEM(table.shape, jnp.bfloat16),
            dma((8,)),
            pltpu.VMEM((rows, tables // 2, samples, 2 * bag_size), jnp.int32),
            pltpu.VMEM((depths, rows, tables, samples, rows_dev), f32),
            pltpu.VMEM((rows,) + block, f32),
            pltpu.VMEM((rows,) + block, f32),
            pltpu.VMEM((depths, rows) + block, f32),
            pltpu.VMEM((tables, rows_dev, depths * rows * samples), jnp.bfloat16),
            pltpu.VMEM(table.shape, f32),
            dma((tables,)),
            dma((rows - 1,)),
            dma((rows,)),
            dma((half - 1,)),
            dma((half,)),
            dma((depths,)),
            dma((rows - 1,)),
            dma((rows,)),
            dma((rows - 1,)),
            dma((rows, half - 1)),
            dma((half, rows)),
            dma((depths, rows)),
        ],
        compiler_params=pltpu.CompilerParams(collective_id=0, **params),
    )(
        table,
        owner.reshape(samples, tables, bag_size),
        local_row,
        lengths.T,
        dense_q,
        labels,
        bottom_w,
        top_w,
    )
    new_table, new_accum, logits = pl.pallas_call(
        update_kernel,
        out_shape=[
            jax.ShapeDtypeStruct(table.shape, f32),
            jax.ShapeDtypeStruct(accum.shape, f32),
            jax.ShapeDtypeStruct(logits.shape, f32),
        ],
        in_specs=[hbm] * 4,
        out_specs=[hbm] * 3,
        scratch_shapes=[
            pltpu.VMEM(table.shape, f32),
            pltpu.VMEM(table.shape, f32),
            pltpu.VMEM(accum.shape, f32),
            pltpu.VMEM(table.shape, f32),
            pltpu.VMEM(accum.shape, f32),
            dma((2 * tables + 2,)),
            dma((tables + 1,)),
        ],
        compiler_params=pltpu.CompilerParams(vmem_limit_bytes=63 * 1024 * 1024),
    )(row_grad, table, accum, logits)
    return new_table, new_accum, logits.reshape(samples)


def by_size(table, *rest):
    tables, _, features = table.shape
    samples = rest[1].shape[0]
    devices = lax.axis_size("row") * lax.axis_size("depth")
    gathered = devices * samples * tables * features * 4
    if gathered <= 4 * 1024 * 1024:
        return shards_small(table, *rest)
    return shards_large(table, *rest)


def solution(mesh):
    in_specs = (
        P(None, "row", None),
        P(None, "row"),
        P(("row", "depth"), None, None, None),
        P(("row", "depth"), None, None),
        P(("row", "depth"), None),
        P(("row", "depth"), None),
        P(("row", "depth")),
        P(),
        P(),
    )
    out_specs = (P(None, "row", None), P(None, "row"), P(("row", "depth")))
    return jax.shard_map(by_size, mesh=mesh, in_specs=in_specs, out_specs=out_specs, check_vma=False)
```

```python
import functools

import jax
import jax.numpy as jnp
import numpy as np
from jax import lax
from jax.experimental import pallas as pl
from jax.experimental.pallas import tpu as pltpu
from jax.sharding import PartitionSpec as P

LEARN_RATE = 0.5
EPSILON = 1e-08


def pair_matrix(top_w, count):
    upper_i, upper_k = np.triu_indices(count, 1)
    matrix = jnp.zeros((count, count), jnp.float32)
    matrix = matrix.at[upper_i, upper_k].set(top_w)
    return matrix.at[upper_k, upper_i].set(top_w)


def adagrad(rows_now, state_now, gradient):
    state = state_now + jnp.mean(gradient * gradient, axis=1)
    return (rows_now - LEARN_RATE * gradient / (jnp.sqrt(state)[:, None] + EPSILON), state)


def shards_large(table, accum, owner, local_row, lengths, dense_q, labels, bottom_w, top_w):
    tables, rows_dev, features = table.shape
    samples, bag_size = (owner.shape[0], owner.shape[2])
    row_devices = lax.axis_size("row")
    slot_count = samples * tables * bag_size
    bag_count = samples * tables
    capacity = 2 * slot_count // row_devices
    row_span = tables * rows_dev
    owner_of = owner.reshape(slot_count)
    local_of = local_row.reshape(slot_count)
    slot_live = (
        lax.broadcasted_iota(jnp.int32, (samples, tables, bag_size), 2) < lengths[:, :, None]
    ).reshape(slot_count)
    slot_index = jnp.arange(slot_count, dtype=jnp.int32)
    bag_of = slot_index // bag_size
    table_of = bag_of % tables
    entry_codes = jnp.where(slot_live, bag_of * row_span + table_of * rows_dev + local_of, -1)
    owner_hits = (owner_of[:, None] == jnp.arange(row_devices, dtype=jnp.int32)[None, :]).astype(
        jnp.int32
    )
    before = jnp.cumsum(owner_hits, axis=0) - owner_hits
    position = jnp.sum(before * owner_hits, axis=1)
    outgoing = (
        jnp.full((row_devices * capacity,), -1, jnp.int32)
        .at[owner_of * capacity + position]
        .set(entry_codes)
    )
    received = lax.all_to_all(
        outgoing.reshape(row_devices, capacity), "row", split_axis=0, concat_axis=0, tiled=True
    )
    is_live = received >= 0
    flat_rows = jnp.where(is_live, received % row_span, 0)
    bag_at = jnp.where(is_live, received // row_span, -1)
    flat_table = table.reshape(row_span, features)
    picked = flat_table[flat_rows]
    choose = (bag_at[:, None, :] == jnp.arange(bag_count, dtype=jnp.int32)[None, :, None]).astype(
        jnp.float32
    )
    partial_pool = jnp.einsum("sbc,scw->sbw", choose, picked, precision=lax.Precision.HIGHEST)
    returned = lax.all_to_all(partial_pool, "row", split_axis=0, concat_axis=0, tiled=True)
    pooled = jnp.sum(returned, axis=0).reshape(samples, tables, features)
    dequant = (dense_q.astype(jnp.float32) - 128.0) / 64.0
    dense_vec = jnp.dot(dequant, bottom_w, precision=lax.Precision.HIGHEST)
    bag_scale = float(bag_size) ** (-0.5)
    width_scale = float(features) ** (-0.5)
    vectors = jnp.concatenate([dense_vec[:, None, :], bag_scale * pooled], axis=1)
    dots = width_scale * jnp.einsum(
        "biw,bkw->bik", vectors, vectors, precision=lax.Precision.HIGHEST
    )
    matrix = pair_matrix(top_w, tables + 1)
    logits = 0.5 * jnp.sum(dots * matrix[None, :, :], axis=(1, 2))
    loss_coeff = (jax.nn.sigmoid(logits) - labels.astype(jnp.float32)) * bag_scale * width_scale
    mixed = jnp.einsum("ti,biw->btw", matrix[1:, :], vectors, precision=lax.Precision.HIGHEST)
    pooled_grad = (loss_coeff[:, None, None] * mixed).reshape(1, bag_count, features)
    piece = lax.all_gather(pooled_grad, "row", axis=0, tiled=True)
    piece_sources = piece.shape[0]
    piece_live = received >= 0
    piece_bags = jnp.where(piece_live, received // row_span, 0)
    source_at = jnp.arange(piece_sources, dtype=jnp.int32)[:, None]
    slot_grads = piece[source_at, piece_bags] * piece_live[:, :, None].astype(jnp.float32)
    row_grad = (
        jnp.zeros((row_span, features), jnp.float32)
        .at[flat_rows.reshape(-1)]
        .add(slot_grads.reshape(-1, features))
    )
    flat_accum = accum.reshape(row_span)
    summed = lax.psum(row_grad, "depth")
    new_rows, new_state = adagrad(flat_table, flat_accum, summed)
    return (
        new_rows.reshape(tables, rows_dev, features),
        new_state.reshape(tables, rows_dev),
        logits,
    )


def remote(src, dst, send_sem, recv_sem, device):
    return pltpu.make_async_remote_copy(
        src_ref=src,
        dst_ref=dst,
        send_sem=send_sem,
        recv_sem=recv_sem,
        device_id=device,
        device_id_type=pl.DeviceIdType.MESH,
    )


def two_terms(value):
    high = value.astype(jnp.bfloat16)
    return high, (value - high.astype(jnp.float32)).astype(jnp.bfloat16)


def matmul(a, b):
    return lax.dot_general(a, b, (((1,), (0,)), ((), ())), preferred_element_type=jnp.float32)


def step_kernel(
    table_in,
    owner_in,
    local_in,
    lengths_in,
    dense_in,
    labels_in,
    bottom_in,
    top_in,
    row_grad_out,
    logits_out,
    table,
    owner,
    local_row,
    lengths,
    dense_q,
    labels,
    bottom_w,
    top_w,
    table_high,
    table_low,
    fetch,
    codes,
    counts,
    partials,
    pools,
    grads,
    weights,
    row_grad,
    logit_row,
    store,
    code_send,
    code_recv,
    count_send,
    count_pass,
    count_recv,
    pool_send,
    pool_recv,
    grad_send,
    grad_spread,
    grad_pass,
    grad_recv,
):
    rows = codes.shape[0]
    depths = counts.shape[0]
    half = depths // 2
    tables, rows_dev, features = table.shape
    samples, _, bag_size = owner.shape
    r = lax.axis_index("row")
    d = lax.axis_index("depth")
    partner = d + 1 - 2 * lax.rem(d, 2)
    row_peers = [lax.rem(r + k, rows) for k in range(1, rows)]
    depth_peers = [lax.rem(d + 2 * k, depths) for k in range(1, half)]
    partner_side = [partner] + [lax.rem(partner + 2 * k, depths) for k in range(1, half)]

    barrier = pltpu.get_barrier_semaphore()
    for peer in row_peers:
        pl.semaphore_signal(
            barrier, inc=1, device_id={"row": peer}, device_id_type=pl.DeviceIdType.MESH
        )
    for peer in depth_peers + [partner]:
        pl.semaphore_signal(
            barrier, inc=1, device_id={"depth": peer}, device_id_type=pl.DeviceIdType.MESH
        )

    fetches = [
        pltpu.make_async_copy(source, target, fetch.at[i])
        for i, (source, target) in enumerate(
            [
                (owner_in, owner),
                (local_in, local_row),
                (lengths_in, lengths),
                (table_in, table),
                (dense_in, dense_q),
                (labels_in, labels),
                (bottom_in, bottom_w),
                (top_in, top_w),
            ]
        )
    ]
    for copy in fetches:
        copy.start()
    eye = lax.broadcasted_iota(jnp.int32, (samples, samples), 0) == lax.broadcasted_iota(
        jnp.int32, (samples, samples), 1
    )
    for copy in fetches[:3]:
        copy.wait()

    slot_at = lax.broadcasted_iota(jnp.int32, (samples, bag_size), 1).astype(jnp.float32)
    lengths_f = lengths[...].astype(jnp.float32)
    mine = []
    for t in range(tables):
        live = slot_at < jnp.sum(jnp.where(eye, lengths_f[t : t + 1, :], 0.0), axis=1, keepdims=True)
        mine.append(jnp.where(live, owner[:, t, :] * rows_dev + local_row[:, t, :], -1))
    for p in range(tables // 2):
        codes[r, p] = jnp.concatenate([mine[2 * p], mine[2 * p + 1]], axis=1)

    row_at = lax.broadcasted_iota(jnp.int32, (samples, rows_dev), 1)

    def count(source):
        def pair(p, carry):
            relative = codes[source, p] - r * rows_dev
            for side in range(2):
                total = jnp.zeros((samples, rows_dev), jnp.float32)
                for j in range(bag_size):
                    at = side * bag_size + j
                    total = total + jnp.where(relative[:, at : at + 1] == row_at, 1.0, 0.0)
                counts[d, source, 2 * p + side] = total
            return carry

        lax.fori_loop(0, tables // 2, pair, 0)

    def pool_copy(k, source):
        return remote(
            partials.at[source], pools.at[r], pool_send.at[k], pool_recv.at[r], {"row": source}
        )

    def pool(source, target):
        for t in range(tables):
            chosen = counts[d, source, t].astype(jnp.bfloat16)
            target[source, t] = matmul(chosen, table_high[t]) + matmul(chosen, table_low[t])

    count(r)
    for copy in fetches[3:]:
        copy.wait()
    for t in range(tables):
        table_high[t], table_low[t] = two_terms(table[t])

    pl.semaphore_wait(barrier, rows - 1 + half)

    code_copies = [
        remote(codes.at[r], codes.at[r], code_send.at[i], code_recv.at[r], {"row": peer})
        for i, peer in enumerate(row_peers)
    ]
    for copy in code_copies:
        copy.start()

    def count_peer(k, carry):
        source = lax.rem(r + k, rows)
        remote(
            codes.at[source], codes.at[source], code_send.at[0], code_recv.at[source], {"row": source}
        ).wait_recv()
        count(source)
        pool(source, partials)
        pool_copy(k - 1, source).start()
        return carry

    lax.fori_loop(1, rows, count_peer, 0)

    count_copies = [
        remote(counts.at[d], counts.at[d], count_send.at[i], count_recv.at[d], {"depth": peer})
        for i, peer in enumerate(depth_peers)
    ]

    pool_copies = [pool_copy(i, peer) for i, peer in enumerate(row_peers)]
    for copy in count_copies:
        copy.start()
    passed = [
        remote(counts.at[d], counts.at[d], count_pass.at[0], count_recv.at[d], {"depth": partner})
    ]
    passed[0].start()
    pool(r, pools)

    dequant = (dense_q[...].astype(jnp.float32) - 128.0) / 64.0
    dense_vec = jnp.zeros((samples, features), jnp.float32)
    for i in range(bottom_w.shape[0]):
        dense_vec = dense_vec + dequant[:, i : i + 1] * bottom_w[i : i + 1, :]
    label_col = jnp.zeros((samples, 1), jnp.float32)
    sample_at = lax.broadcasted_iota(jnp.int32, (samples, 1), 0)
    for b in range(samples):
        label_col = jnp.where(sample_at == b, labels[b].astype(jnp.float32), label_col)
    for peer in row_peers:
        remote(
            pools.at[peer], pools.at[peer], pool_send.at[0], pool_recv.at[peer], {"row": peer}
        ).wait_recv()

    bag_scale = float(bag_size) ** (-0.5)
    width_scale = float(features) ** (-0.5)
    vectors = [dense_vec] + [bag_scale * jnp.sum(pools[:, t], axis=0) for t in range(tables)]
    pair_at = {}
    for i in range(tables + 1):
        for k in range(i + 1, tables + 1):
            pair_at[i, k] = pair_at[k, i] = len(pair_at) // 2
    mixed = []
    for i in range(tables + 1):
        terms = [top_w[pair_at[i, k]] * vectors[k] for k in range(tables + 1) if k != i]
        mixed.append(functools.reduce(jnp.add, terms))
    joined = functools.reduce(jnp.add, [vectors[i] * mixed[i] for i in range(tables + 1)])
    logit = (0.5 * width_scale) * jnp.sum(joined, axis=1, keepdims=True)
    coeff = (1.0 / (1.0 + jnp.exp(-logit)) - label_col) * (bag_scale * width_scale)
    for t in range(tables):
        grads[d, r, t] = coeff * mixed[1 + t]

    grad_copies = []
    for i, peer in enumerate(row_peers):
        grad_copies.append(
            remote(
                grads.at[d, r], grads.at[d, r], grad_send.at[i], grad_recv.at[d, r], {"row": peer}
            )
        )

    def spread(n, row):
        made = [
            remote(
                grads.at[d, row],
                grads.at[d, row],
                grad_spread.at[n, i],
                grad_recv.at[d, row],
                {"depth": peer},
            )
            for i, peer in enumerate(depth_peers)
        ]
        made.append(pass_on(0, n, d, row))
        for copy in made:
            copy.start()
        return made

    def pass_on(m, n, depth, row):
        return remote(
            grads.at[depth, row],
            grads.at[depth, row],
            grad_pass.at[m, n],
            grad_recv.at[depth, row],
            {"depth": partner},
        )

    for copy in grad_copies:
        copy.start()
    grad_copies += spread(0, r)

    logit_row[...] = jnp.sum(jnp.where(eye, logit, 0.0), axis=0, keepdims=True)
    logits_copy = pltpu.make_async_copy(logit_row, logits_out, store.at[tables])
    logits_copy.start()

    for n, peer in enumerate(row_peers):
        remote(
            grads.at[d, peer], grads.at[d, peer], grad_send.at[0], grad_recv.at[d, peer], {"row": peer}
        ).wait_recv()
        grad_copies += spread(n + 1, peer)

    for m, peer in enumerate(depth_peers):
        remote(
            counts.at[peer], counts.at[peer], count_send.at[0], count_recv.at[peer], {"depth": peer}
        ).wait_recv()
        copy = remote(
            counts.at[peer],
            counts.at[peer],
            count_pass.at[m + 1],
            count_recv.at[peer],
            {"depth": partner},
        )
        copy.start()
        passed.append(copy)

    for n, row in enumerate([r] + row_peers):
        for m, peer in enumerate(depth_peers):
            remote(
                grads.at[peer, row],
                grads.at[peer, row],
                grad_send.at[0],
                grad_recv.at[peer, row],
                {"depth": peer},
            ).wait_recv()
            copy = pass_on(m + 1, n, peer, row)
            copy.start()
            grad_copies.append(copy)

    for peer in partner_side:
        remote(
            counts.at[peer], counts.at[peer], count_send.at[0], count_recv.at[peer], {"depth": partner}
        ).wait_recv()
    batch = depths * rows * samples
    for t in range(tables):
        weights[t] = counts[:, :, t].reshape(batch, rows_dev).T.astype(jnp.bfloat16)

    for copy in code_copies + count_copies + passed + pool_copies:
        copy.wait_send()
    logits_copy.wait()
    for row in [r] + row_peers:
        for peer in partner_side:
            remote(
                grads.at[peer, row],
                grads.at[peer, row],
                grad_send.at[0],
                grad_recv.at[peer, row],
                {"depth": partner},
            ).wait_recv()

    for t in range(tables):
        high, low = two_terms(grads[:, :, t].reshape(batch, features))
        row_grad[t] = matmul(weights[t], high) + matmul(weights[t], low)
        pltpu.make_async_copy(row_grad.at[t], row_grad_out.at[t], store.at[t]).start()

    for copy in grad_copies:
        copy.wait_send()
    for t in range(tables):
        pltpu.make_async_copy(row_grad.at[t], row_grad_out.at[t], store.at[t]).wait()


def update_kernel(
    grad_in,
    table_in,
    accum_in,
    logits_in,
    new_table,
    new_accum,
    logits_out,
    grad,
    table,
    accum,
    result,
    state_rows,
    fetch,
    store,
):
    tables, rows_dev, features = table.shape
    first = [
        pltpu.make_async_copy(accum_in, accum, fetch.at[2 * tables]),
        pltpu.make_async_copy(logits_in, logits_out, fetch.at[2 * tables + 1]),
    ]
    blocks = [
        (
            pltpu.make_async_copy(grad_in.at[t], grad.at[t], fetch.at[2 * t]),
            pltpu.make_async_copy(table_in.at[t], table.at[t], fetch.at[2 * t + 1]),
        )
        for t in range(tables)
    ]
    stores = [
        pltpu.make_async_copy(result.at[t], new_table.at[t], store.at[t]) for t in range(tables)
    ]
    stores.append(pltpu.make_async_copy(state_rows, new_accum, store.at[tables]))
    for copy in first:
        copy.start()
    for pair in blocks:
        for copy in pair:
            copy.start()
    diagonal = lax.broadcasted_iota(jnp.int32, (rows_dev, rows_dev), 0) == lax.broadcasted_iota(
        jnp.int32, (rows_dev, rows_dev), 1
    )
    first[0].wait()
    before = [
        jnp.sum(jnp.where(diagonal, accum[t : t + 1, :], 0.0), axis=1, keepdims=True)
        for t in range(tables)
    ]
    for t in range(tables):
        for copy in blocks[t]:
            copy.wait()
        row_grad = grad[t]
        state = before[t] + jnp.sum(row_grad * row_grad, axis=1, keepdims=True) / features
        result[t] = table[t] - row_grad * (LEARN_RATE / (jnp.sqrt(state) + EPSILON))
        stores[t].start()
        state_rows[t : t + 1, :] = jnp.sum(
            jnp.where(diagonal, state, 0.0), axis=0, keepdims=True
        )
    stores[tables].start()
    first[1].wait()
    for copy in stores:
        copy.wait()


def shards_small(table, accum, owner, local_row, lengths, dense_q, labels, bottom_w, top_w):
    tables, rows_dev, features = table.shape
    samples, bag_size = (owner.shape[0], owner.shape[2])
    rows = lax.axis_size("row")
    depths = lax.axis_size("depth")
    half = depths // 2
    f32 = jnp.float32
    dma = pltpu.SemaphoreType.DMA
    hbm = pl.BlockSpec(memory_space=pltpu.HBM)
    i32 = jnp.int32
    block = (tables, samples, features)
    params = dict(has_side_effects=True, vmem_limit_bytes=63 * 1024 * 1024)
    row_grad, logits = pl.pallas_call(
        step_kernel,
        out_shape=[
            jax.ShapeDtypeStruct(table.shape, f32),
            jax.ShapeDtypeStruct((1, samples), f32),
        ],
        in_specs=[hbm] * 8,
        out_specs=[hbm, hbm],
        scratch_shapes=[
            pltpu.VMEM(table.shape, f32),
            pltpu.VMEM((samples, tables, bag_size), i32),
            pltpu.VMEM(local_row.shape, i32),
            pltpu.VMEM((tables, samples), i32),
            pltpu.VMEM(dense_q.shape, i32),
            pltpu.SMEM(labels.shape, i32),
            pltpu.VMEM(bottom_w.shape, f32),
            pltpu.SMEM(top_w.shape, f32),
            pltpu.VMEM(table.shape, jnp.bfloat16),
            pltpu.VMEM(table.shape, jnp.bfloat16),
            dma((8,)),
            pltpu.VMEM((rows, tables // 2, samples, 2 * bag_size), jnp.int32),
            pltpu.VMEM((depths, rows, tables, samples, rows_dev), f32),
            pltpu.VMEM((rows,) + block, f32),
            pltpu.VMEM((rows,) + block, f32),
            pltpu.VMEM((depths, rows) + block, f32),
            pltpu.VMEM((tables, rows_dev, depths * rows * samples), jnp.bfloat16),
            pltpu.VMEM(table.shape, f32),
            pltpu.VMEM((1, samples), f32),
            dma((tables + 1,)),
            dma((rows - 1,)),
            dma((rows,)),
            dma((half - 1,)),
            dma((half,)),
            dma((depths,)),
            dma((rows - 1,)),
            dma((rows,)),
            dma((rows - 1,)),
            dma((rows, half - 1)),
            dma((half, rows)),
            dma((depths, rows)),
        ],
        compiler_params=pltpu.CompilerParams(collective_id=0, **params),
    )(
        table,
        owner.reshape(samples, tables, bag_size),
        local_row,
        lengths.T,
        dense_q,
        labels,
        bottom_w,
        top_w,
    )
    new_table, new_accum, logits = pl.pallas_call(
        update_kernel,
        out_shape=[
            jax.ShapeDtypeStruct(table.shape, f32),
            jax.ShapeDtypeStruct(accum.shape, f32),
            jax.ShapeDtypeStruct(logits.shape, f32),
        ],
        in_specs=[hbm] * 4,
        out_specs=[hbm] * 3,
        scratch_shapes=[
            pltpu.VMEM(table.shape, f32),
            pltpu.VMEM(table.shape, f32),
            pltpu.VMEM(accum.shape, f32),
            pltpu.VMEM(table.shape, f32),
            pltpu.VMEM(accum.shape, f32),
            dma((2 * tables + 2,)),
            dma((tables + 1,)),
        ],
        compiler_params=pltpu.CompilerParams(vmem_limit_bytes=63 * 1024 * 1024),
    )(row_grad, table, accum, logits)
    return new_table, new_accum, logits.reshape(samples)


def by_size(table, *rest):
    tables, _, features = table.shape
    samples = rest[1].shape[0]
    devices = lax.axis_size("row") * lax.axis_size("depth")
    gathered = devices * samples * tables * features * 4
    if gathered <= 4 * 1024 * 1024:
        return shards_small(table, *rest)
    return shards_large(table, *rest)


def solution(mesh):
    in_specs = (
        P(None, "row", None),
        P(None, "row"),
        P(("row", "depth"), None, None, None),
        P(("row", "depth"), None, None),
        P(("row", "depth"), None),
        P(("row", "depth"), None),
        P(("row", "depth")),
        P(),
        P(),
    )
    out_specs = (P(None, "row", None), P(None, "row"), P(("row", "depth")))
    return jax.shard_map(by_size, mesh=mesh, in_specs=in_specs, out_specs=out_specs, check_vma=False)
```
